768 devices in a mesh: seq: 96 (over x, z, core), head: 8 (over y).
Axes of the slice: x: 4, y: 8, z: 12, core: 2. Of those that a mesh axis runs over, the one named last changes fastest.
Arguments:
- queries: bfloat16 [12288, 16, 128], P('seq', 'head'), may hold values from -6 to 6
- keys: bfloat16 [12288, 16, 128], P('seq', 'head'), may hold values from -1.5 to 1.5
- values: bfloat16 [12288, 16, 128], P('seq', 'head'), may hold values from -6 to 6
- reg: float32 [16], P('head'), may hold values from 1 to 8
- steps: int32 [96, 16], P('seq', 'head'), may hold values from 1 to 12, as said below
- w_out: bfloat16 [2048, 2048], P('head'), may hold values from -0.125 to 0.125
- d_y: bfloat16 [12288, 2048], P(('seq', 'head')), may hold values from -6 to 6
Outputs:
- out: bfloat16 [12288, 2048], P(('seq', 'head'))
- grad_queries: bfloat16 [12288, 16, 128], P('seq', 'head')
- grad_keys: bfloat16 [12288, 16, 128], P('seq', 'head')
- grad_values: bfloat16 [12288, 16, 128], P('seq', 'head')
The draws below stay inside these ranges and needn't reach their ends.
Inputs may be any that keep to these rules, and one draw needn't show every extreme that they name: steps[b, h] counts the conjugate-gradient steps of block b of 128 tokens and head h; some entry equals 12 in every draw.
All inputs are finite; a program needn't handle non-finite values.
Results may differ from the reference program's by a relative error of at most 0.022.
Values may be sent and summed in bfloat16 or wider, within the bound.
No kernel may reach another device: no remote copies, remote signals or barrier semaphores. Data moves between devices by JAX's collectives and lax.ppermute only.
A program may use at most 128 MiB of HBM per device.

```python
import math
import jax
import jax.numpy as jnp
from jax import lax

HEADS = 16
DH = 128
TOK_DEV = 128
STEPS_MAX = 12
SPANS = 96
TOKENS = 12288
D = 2048


def draw_keys(key, part):
    scale_key, entry_key = jax.random.split(jax.random.fold_in(key, 11), 2)
    channel_scale = jnp.exp(jax.random.uniform(scale_key, (HEADS, DH), jnp.float32, math.log(0.03), math.log(0.3)))
    entries = jnp.clip(jax.random.normal(entry_key, (TOKENS, HEADS, DH), jnp.float32), -5.0, 5.0)
    return (entries * channel_scale).astype(jnp.bfloat16)


def draw_steps(key, part):
    base_key, heavy_key, forced_key = jax.random.split(jax.random.fold_in(key, 23), 3)
    counts = jax.random.randint(base_key, (SPANS, HEADS), 1, 10)
    heavy_mask = jax.random.randint(heavy_key, (SPANS, HEADS), 0, 16) == 0
    counts = jnp.where(heavy_mask, STEPS_MAX, counts)
    forced_at = jax.random.randint(forced_key, (), 0, SPANS * HEADS)
    flat_counts = counts.reshape(-1)
    flat_counts = jnp.where(jnp.arange(SPANS * HEADS) == forced_at, STEPS_MAX, flat_counts)
    return flat_counts.reshape(SPANS, HEADS).astype(jnp.int32)


def shard_levels(own_key, dims, cuts, least, top_value):
    def one(position, parts):
        heights = jax.random.uniform(jax.random.fold_in(jax.random.fold_in(own_key, 6), position), (parts,), jnp.float32, least / len(cuts), top_value / len(cuts))
        return jnp.repeat(jnp.exp(heights), dims[position] // parts).reshape((-1,) + (1,) * (len(dims) - position - 1))

    loudness = one(*cuts[0])
    for cut in cuts[1:]:
        loudness = loudness * one(*cut)
    return loudness


def scatter_about(key, shape, width, most, shards=(), held_as=jnp.bfloat16):
    level = shard_levels(key, shape, shards, -0.22, 0.18) if shards else 1.0
    values = jax.random.normal(key, shape, jnp.float32) * width * level
    return jnp.minimum(jnp.maximum(values, -most), most).astype(held_as)


def setup_inputs(seed: int = 0) -> dict:
    streams_of = jax.random.split(jax.random.key(seed), 8)
    queries = scatter_about(streams_of[0], (TOKENS, HEADS, DH), 1.0, 6.0, ((0, 96), (1, 8)))
    keys = draw_keys(jax.random.fold_in(streams_of[7], 71), 0)
    values = scatter_about(streams_of[2], (TOKENS, HEADS, DH), 1.0, 6.0, ((0, 96), (1, 8)))
    reg = jnp.clip(jnp.exp(math.log(8.0) - 2.0794415 * jax.random.uniform(streams_of[3], (HEADS,), jnp.float32) ** shard_levels(streams_of[3], (HEADS,), ((0, 8),), -0.2, 0.2)), 1.0, 8.0)
    steps = draw_steps(jax.random.fold_in(streams_of[7], 71), 0)
    w_out = scatter_about(streams_of[5], (D, D), D ** -0.5, 0.125, ((0, 8),))
    d_y = scatter_about(streams_of[6], (TOKENS, D), 1.0, 6.0, ((0, 768),))
    return {"queries": queries, "keys": keys, "values": values, "reg": reg, "steps": steps, "w_out": w_out, "d_y": d_y}


epsilon = 1e-6
highest = lax.Precision.HIGHEST


def apply_cov(direction, key_rows, cov_prev, ridge, causal_low):
    result = jnp.einsum('hsd,hde->hse', direction, cov_prev, precision=highest)
    scores = jnp.einsum('hsd,htd->hst', direction, key_rows, precision=highest) * causal_low
    result = result + jnp.einsum('hst,htd->hsd', scores, key_rows, precision=highest)
    return result + ridge[:, None, None] * direction


def cg_solve(right, key_rows, cov_prev, ridge, counts, causal_low):
    def cg_step(step_idx, cg_state):
        sol, resid, direction, resid_sq = cg_state
        image = apply_cov(direction, key_rows, cov_prev, ridge, causal_low)
        step_len = resid_sq / (jnp.sum(direction * image, -1, keepdims=True) + epsilon)
        sol_new = sol + step_len * direction
        resid_new = resid - step_len * image
        sq_new = jnp.sum(resid_new * resid_new, -1, keepdims=True)
        dir_new = resid_new + (sq_new / (resid_sq + epsilon)) * direction
        live_mask = (step_idx < counts)[:, None, None]
        return (jnp.where(live_mask, sol_new, sol), jnp.where(live_mask, resid_new, resid),
                jnp.where(live_mask, dir_new, direction), jnp.where(live_mask, sq_new, resid_sq))

    start_state = (jnp.zeros_like(right), right, right, jnp.sum(right * right, -1, keepdims=True))
    return lax.fori_loop(0, STEPS_MAX, cg_step, start_state)[0]


def reference(queries, keys, values, reg, steps, w_out, d_y):
    size_c = TOK_DEV

    def heads_first(array):
        return array.reshape(SPANS, size_c, HEADS, DH).transpose(0, 2, 1, 3).astype(jnp.float32)

    query_h, key_h, value_h = heads_first(queries), heads_first(keys), heads_first(values)
    back_all = lax.dot_general(d_y, w_out, (((1,), (1,)), ((), ())), preferred_element_type=jnp.float32)
    back_h = heads_first(back_all)
    positions = jnp.arange(size_c)
    causal_low = (positions[:, None] >= positions[None, :]).astype(jnp.float32)
    causal_up = (positions[:, None] <= positions[None, :]).astype(jnp.float32)

    def forward(running, inputs):
        cov_prev, state_prev = running
        key_rows, val_rows, qry_rows, back_rows, counts = inputs
        sol = cg_solve(qry_rows, key_rows, cov_prev, reg, counts, causal_low)
        scores = jnp.einsum('hck,htk->hct', sol, key_rows, precision=highest) * causal_low
        mixed = jnp.einsum('hck,hvk->hcv', sol, state_prev, precision=highest)
        mixed = mixed + jnp.einsum('hct,htv->hcv', scores, val_rows, precision=highest)
        scores_b = jnp.einsum('hcv,htv->hct', back_rows, val_rows, precision=highest) * causal_low
        adjoint = jnp.einsum('hcv,hvk->hck', back_rows, state_prev, precision=highest)
        adjoint = adjoint + jnp.einsum('hct,htk->hck', scores_b, key_rows, precision=highest)
        dual = cg_solve(adjoint, key_rows, cov_prev, reg, counts, causal_low)
        cov_next = cov_prev + jnp.einsum('hcd,hce->hde', key_rows, key_rows, precision=highest)
        state_next = state_prev + jnp.einsum('hcv,hck->hvk', val_rows, key_rows, precision=highest)
        return (cov_next, state_next), (sol, dual, mixed.astype(jnp.bfloat16))

    zero_mats = jnp.zeros((HEADS, DH, DH), jnp.float32)
    _, (sol_all, dual_all, mixed_all) = lax.scan(forward, (zero_mats, zero_mats),
                                                 (key_h, value_h, query_h, back_h, steps))

    def backward(running, inputs):
        sym_sum, cross_sum = running
        key_rows, val_rows, sol, dual, back_rows = inputs
        m_one = jnp.einsum('hid,hsd->his', key_rows, sol, precision=highest) * causal_up
        m_two = jnp.einsum('hid,hsd->his', key_rows, dual, precision=highest) * causal_up
        m_three = jnp.einsum('hiv,hsv->his', val_rows, back_rows, precision=highest) * causal_up
        neg_part = jnp.einsum('hie,hde->hid', key_rows, sym_sum, precision=highest)
        neg_part = neg_part + jnp.einsum('his,hsd->hid', m_one, dual, precision=highest)
        neg_part = neg_part + jnp.einsum('his,hsd->hid', m_two, sol, precision=highest)
        grad_k = jnp.einsum('hiv,hvk->hik', val_rows, cross_sum, precision=highest)
        grad_k = grad_k + jnp.einsum('his,hsk->hik', m_three, sol, precision=highest) - neg_part
        grad_v = jnp.einsum('hik,hvk->hiv', key_rows, cross_sum, precision=highest)
        grad_v = grad_v + jnp.einsum('his,hsv->hiv', m_one, back_rows, precision=highest)
        outer_sum = jnp.einsum('hsd,hse->hde', dual, sol, precision=highest)
        sym_next = sym_sum + outer_sum + jnp.swapaxes(outer_sum, 1, 2)
        cross_next = cross_sum + jnp.einsum('hsv,hsk->hvk', back_rows, sol, precision=highest)
        return (sym_next, cross_next), (grad_k.astype(jnp.bfloat16), grad_v.astype(jnp.bfloat16))

    _, (grad_k_all, grad_v_all) = lax.scan(backward, (zero_mats, zero_mats),
                                           (key_h, value_h, sol_all, dual_all, back_h), reverse=True)

    def tokens_first(array):
        return array.transpose(0, 2, 1, 3).reshape(TOKENS, HEADS, DH)

    mixed_flat = tokens_first(mixed_all).reshape(TOKENS, D)
    out = jnp.dot(mixed_flat, w_out, preferred_element_type=jnp.float32).astype(jnp.bfloat16)
    grad_queries = tokens_first(dual_all).astype(jnp.bfloat16)
    return (out, grad_queries, tokens_first(grad_k_all), tokens_first(grad_v_all))
```

```python
import functools
import jax
import jax.numpy as jnp
from jax import lax
from jax.experimental import pallas as pl
from jax.experimental.pallas import tpu as pltpu
from jax.sharding import PartitionSpec as P

STEPS_MAX = 12
epsilon = 1e-06
f32 = jnp.float32
bf16 = jnp.bfloat16
N_DIMS = (((1,), (0,)), ((), ()))
T_DIMS = (((1,), (1,)), ((), ()))
L_DIMS = (((0,), (0,)), ((), ()))


def dot(a, b, dims=N_DIMS):
    return lax.dot_general(a, b, dims, preferred_element_type=f32)


def halves(a):
    high = a.astype(bf16)
    return high, (a - high.astype(f32)).astype(bf16)


def wide(a):
    return jnp.concatenate(halves(a), axis=1)


def twice(b):
    return jnp.concatenate([b, b], axis=0)


def causal(rows, transposed=False):
    r = lax.rem(lax.broadcasted_iota(jnp.int32, (rows, 128), 0), 128)
    c = lax.broadcasted_iota(jnp.int32, (rows, 128), 1)
    return (r <= c) if transposed else (r >= c)


def pack(mats, out_ref):
    spans = out_ref.shape[0]
    stack = jnp.concatenate(mats, axis=0).astype(bf16)
    groups = out_ref.shape[1] // 128
    for g in range(groups):
        lo, hi = g * spans, min((g + 1) * spans, 512)
        out_ref[0 : hi - lo, g * 128 : (g + 1) * 128] = stack[lo:hi]
        if hi - lo < spans:
            out_ref[hi - lo : spans, g * 128 : (g + 1) * 128] = jnp.zeros(
                (spans - (hi - lo), 128), bf16
            )


def unpack(ref):
    groups = ref.shape[1] // 128
    stack = jnp.concatenate([ref[:, g * 128 : (g + 1) * 128] for g in range(groups)], axis=0)
    return [stack[i * 128 : (i + 1) * 128] for i in range(4)]


def own_kernel(k_ref, v_ref, out_ref):
    k, v = k_ref[...], v_ref[...]
    mats = []
    for h in range(2):
        mats.append(dot(k[:, h * 128 : (h + 1) * 128], k[:, h * 128 : (h + 1) * 128], L_DIMS))
    for h in range(2):
        mats.append(dot(v[:, h * 128 : (h + 1) * 128], k[:, h * 128 : (h + 1) * 128], L_DIMS))
    pack(mats, out_ref)


def scan_kernel(later, x_ref, out_ref):
    n = x_ref.shape[0]
    r = lax.broadcasted_iota(jnp.int32, (n, n), 0)
    c = lax.broadcasted_iota(jnp.int32, (n, n), 1)
    tri = jnp.where((c > r) if later else (c < r), 1.0, 0.0).astype(bf16)
    out_ref[...] = dot(tri, x_ref[...]).astype(bf16)


def solve_kernel(
    steps_ref,
    reg_ref,
    q_ref,
    k_ref,
    v_ref,
    back_ref,
    pre_ref,
    sol_ref,
    dual_ref,
    mixed_ref,
    grad_q_ref,
    send_ref,
    x_s,
    r_s,
    p_s,
    b_s,
    k_s,
):
    mats = unpack(pre_ref)
    low = causal(128)
    low_two = causal(256)
    for h in range(2):
        lanes = slice(h * 128, (h + 1) * 128)
        k, v, back = k_ref[:, lanes], v_ref[:, lanes], back_ref[:, lanes]
        cov, state = mats[h], mats[2 + h]
        both = jnp.concatenate([cov, k.T], axis=1)
        b_s[h] = twice(both)
        k_s[h] = twice(k)
        firsts = wide(back)
        scores = jnp.where(low, dot(firsts, jnp.concatenate([v, v], axis=1), T_DIMS), 0.0)
        adjoint = dot(firsts, twice(state)) + dot(wide(scores), twice(k))
        right = jnp.concatenate([q_ref[:, lanes].astype(f32), adjoint], axis=0)
        x_s[h] = jnp.zeros_like(right)
        r_s[h] = right
        p_s[h] = right
    rr0 = tuple(jnp.sum(r_s[h] * r_s[h], -1, keepdims=True) for h in range(2))

    def step(i, rrs):
        news = []
        for h in range(2):
            rr = rrs[h]
            p = p_s[h]
            first = dot(wide(p), b_s[h])
            scores = jnp.where(low_two, first[:, 128:], 0.0)
            image = first[:, :128] + dot(wide(scores), k_s[h]) + reg_ref[h] * p
            alpha = rr / (jnp.sum(p * image, -1, keepdims=True) + epsilon)
            kept = jnp.where(i < steps_ref[0, h], alpha, 0.0)
            x_s[h] = x_s[h] + kept * p
            r = r_s[h] - alpha * image
            r_s[h] = r
            new = jnp.sum(r * r, -1, keepdims=True)
            p_s[h] = r + (new / (rr + epsilon)) * p
            news.append(new)
        return tuple(news)

    lax.fori_loop(0, jnp.maximum(steps_ref[0, 0], steps_ref[0, 1]), step, rr0)

    syms, crosses = [], []
    for h in range(2):
        lanes = slice(h * 128, (h + 1) * 128)
        k, v, back = k_ref[:, lanes], v_ref[:, lanes], back_ref[:, lanes]
        state = mats[2 + h]
        sol, dual = x_s[h, :128, :], x_s[h, 128:, :]
        sol_ref[:, lanes] = sol
        dual_ref[:, lanes] = dual
        grad_q_ref[:, lanes] = dual.astype(bf16)
        firsts = wide(sol)
        scores = jnp.where(low, dot(firsts, jnp.concatenate([k, k], axis=1), T_DIMS), 0.0)
        mixed = dot(firsts, jnp.concatenate([state, state], axis=1), T_DIMS) + dot(wide(scores), twice(v))
        mixed_ref[:, lanes] = mixed.astype(bf16)
        sol_high, sol_low = halves(sol)
        dual_high, dual_low = halves(dual)
        back_high, back_low = halves(back)
        outer = dot(
            jnp.concatenate([dual_high, dual_high, dual_low], axis=0),
            jnp.concatenate([sol_high, sol_low, sol_high], axis=0),
            L_DIMS,
        )
        syms.append(outer + outer.T)
        crosses.append(
            dot(
                jnp.concatenate([back_high, back_high, back_low], axis=0),
                jnp.concatenate([sol_high, sol_low, sol_high], axis=0),
                L_DIMS,
            )
        )
    pack(syms + crosses, send_ref)


def inner_kernel(k_ref, v_ref, back_ref, sol_ref, dual_ref, gk_ref, gv_ref):
    up = causal(128, True)
    for h in range(2):
        lanes = slice(h * 128, (h + 1) * 128)
        k, v, back = k_ref[:, lanes], v_ref[:, lanes], back_ref[:, lanes]
        sol, dual = sol_ref[:, lanes], dual_ref[:, lanes]
        kk = jnp.concatenate([k, k], axis=1)
        vv = jnp.concatenate([v, v], axis=1)
        one = wide(jnp.where(up, dot(kk, wide(sol), T_DIMS), 0.0))
        two = wide(jnp.where(up, dot(kk, wide(dual), T_DIMS), 0.0))
        three = wide(jnp.where(up, dot(vv, wide(back), T_DIMS), 0.0))
        sol_b, dual_b, back_b = sol.astype(bf16), dual.astype(bf16), back.astype(bf16)
        gk_ref[:, lanes] = dot(three, twice(sol_b)) - dot(one, twice(dual_b)) - dot(two, twice(sol_b))
        gv_ref[:, lanes] = dot(one, twice(back_b))


def final_kernel(k_ref, v_ref, gk_ref, gv_ref, suf_ref, grad_k_ref, grad_v_ref):
    mats = unpack(suf_ref)
    for h in range(2):
        lanes = slice(h * 128, (h + 1) * 128)
        k, v = k_ref[:, lanes], v_ref[:, lanes]
        sym, cross = mats[h], mats[2 + h]
        grad_k_ref[:, lanes] = (gk_ref[:, lanes] + dot(v, cross) - dot(k, sym)).astype(bf16)
        grad_v_ref[:, lanes] = (gv_ref[:, lanes] + dot(k, cross, T_DIMS)).astype(bf16)


def call(kernel, outs, n_smem=0, n_in=0, scratch=(), flops=0, bytes_accessed=0):
    return pl.pallas_call(
        kernel,
        out_shape=[jax.ShapeDtypeStruct(s, d) for s, d in outs],
        in_specs=[pl.BlockSpec(memory_space=pltpu.SMEM)] * n_smem
        + [pl.BlockSpec(memory_space=pltpu.VMEM)] * n_in,
        out_specs=[pl.BlockSpec(memory_space=pltpu.VMEM)] * len(outs),
        scratch_shapes=list(scratch),
        compiler_params=pltpu.CompilerParams(vmem_limit_bytes=24 * 1024 * 1024),
        cost_estimate=pl.CostEstimate(flops=flops, bytes_accessed=bytes_accessed, transcendentals=0),
    )


def local(queries, keys, values, reg, steps, w_out, d_y):
    size_c, head_count, head_size = queries.shape
    width = head_count * head_size
    spans = lax.axis_size("seq")
    packed = (spans, -(-head_count * 2 * head_size // spans) * head_size)
    tokens = (size_c, width)

    q, k, v = (a.reshape(tokens) for a in (queries, keys, values))

    def exchange(a):
        return lax.all_to_all(a, "seq", 0, 0, tiled=True)

    def scan(a, later):
        return call(functools.partial(scan_kernel, later), [(packed, bf16)], 0, 1)(a)[0]

    (own,) = call(own_kernel, [(packed, bf16)], 0, 2)(k, v)
    dy_rows = lax.all_gather(d_y, "head", axis=0, tiled=True)
    back = lax.dot_general(dy_rows, w_out, T_DIMS, preferred_element_type=f32)
    pre = exchange(scan(exchange(own), False))

    sol, dual, mixed, grad_q, send = call(
        solve_kernel,
        [(tokens, f32), (tokens, f32), (tokens, bf16), (tokens, bf16), (packed, bf16)],
        2,
        5,
        [
            pltpu.VMEM((2, 256, 128), f32),
            pltpu.VMEM((2, 256, 128), f32),
            pltpu.VMEM((2, 256, 128), f32),
            pltpu.VMEM((2, 256, 256), bf16),
            pltpu.VMEM((2, 256, 128), bf16),
        ],
        flops=2 * 10**9,
    )(steps, reg, q, k, v, back, pre)
    out = lax.psum_scatter(
        jnp.dot(mixed, w_out, preferred_element_type=f32).astype(bf16),
        "head",
        scatter_dimension=0,
        tiled=True,
    )
    suf = exchange(scan(exchange(send), True))
    gk, gv = call(inner_kernel, [(tokens, f32), (tokens, f32)], 0, 5, flops=2 * 10**8)(
        k, v, back, sol, dual
    )
    grad_k, grad_v = call(final_kernel, [(tokens, bf16), (tokens, bf16)], 0, 5)(k, v, gk, gv, suf)
    heads = (size_c, head_count, head_size)
    return out, grad_q.reshape(heads), grad_k.reshape(heads), grad_v.reshape(heads)


def solution(mesh):
    placed = (
        P("seq", "head", None),
        P("seq", "head", None),
        P("seq", "head", None),
        P("head"),
        P("seq", "head"),
        P("head", None),
        P(("seq", "head"), None),
    )
    return jax.shard_map(
        local,
        mesh=mesh,
        in_specs=placed,
        out_specs=(
            P(("seq", "head"), None),
            P("seq", "head", None),
            P("seq", "head", None),
            P("seq", "head", None),
        ),
        check_vma=False,
    )
```

```python
import functools
import jax
import jax.numpy as jnp
from jax import lax
from jax.experimental import pallas as pl
from jax.experimental.pallas import tpu as pltpu
from jax.sharding import PartitionSpec as P

STEPS_MAX = 12
epsilon = 1e-06
f32 = jnp.float32
bf16 = jnp.bfloat16
N_DIMS = (((1,), (0,)), ((), ()))
T_DIMS = (((1,), (1,)), ((), ()))
L_DIMS = (((0,), (0,)), ((), ()))


def dot(a, b, dims=N_DIMS):
    return lax.dot_general(a, b, dims, preferred_element_type=f32)


def halves(a):
    high = a.astype(bf16)
    return high, (a - high.astype(f32)).astype(bf16)


def wide(a):
    return jnp.concatenate(halves(a), axis=1)


def twice(b):
    return jnp.concatenate([b, b], axis=0)


def causal(rows, transposed=False):
    r = lax.rem(lax.broadcasted_iota(jnp.int32, (rows, 128), 0), 128)
    c = lax.broadcasted_iota(jnp.int32, (rows, 128), 1)
    return (r <= c) if transposed else (r >= c)


ROWS = 6
STACK = 512


def heads_apart(both):
    head = lax.rem(lax.broadcasted_iota(jnp.int32, (256, 1), 0), 2)
    first = jnp.where(head == 0, 1.0, 0.0).astype(bf16)
    return jnp.concatenate([both * first, both * (1 - first)], axis=1)


def pack(mats, out_ref):
    for i, mat in enumerate(mats):
        out_ref[i * 128 : (i + 1) * 128, :] = mat.astype(bf16)
    rest = out_ref.shape[0] - STACK
    out_ref[STACK:, :] = jnp.zeros((rest, 128), bf16)


def unpack(ref):
    return [ref[i * 128 : (i + 1) * 128, :] for i in range(4)]


def own_kernel(k_ref, v_ref, out_ref):
    k = k_ref[...]
    sums = dot(heads_apart(k), k, L_DIMS)
    states = dot(heads_apart(v_ref[...]), k, L_DIMS)
    pack([sums[:128], sums[128:], states[:128], states[128:]], out_ref)


def scan_kernel(later, x_ref, out_ref):
    n = x_ref.shape[0]

    def place(shape, dim):
        i = lax.broadcasted_iota(jnp.int32, shape, dim)
        span = lax.shift_right_logical(i * 10923, 16)
        return span, i - ROWS * span

    r_span, r_row = place((n, 1), 0)
    c_span, c_row = place((1, n), 1)
    reach = (c_span > r_span) if later else (c_span < r_span)
    tri = jnp.where(reach & (r_row == c_row), 1.0, 0.0).astype(bf16)
    out_ref[...] = dot(tri, x_ref[...]).astype(bf16)


def solve_kernel(
    steps_ref,
    reg_ref,
    q_ref,
    k_ref,
    v_ref,
    back_ref,
    pre_ref,
    sol_ref,
    dual_ref,
    mixed_ref,
    grad_q_ref,
    send_ref,
    x_s,
    r_s,
    p_s,
    b_s,
    k_s,
):
    mats = unpack(pre_ref)
    low = causal(128)
    low_two = causal(256)
    for h in range(2):
        lanes = slice(h * 128, (h + 1) * 128)
        k, v, back = k_ref[:, lanes], v_ref[:, lanes], back_ref[:, lanes]
        cov, state = mats[h], mats[2 + h]
        both = jnp.concatenate([cov, k.T], axis=1)
        b_s[h] = twice(both)
        k_s[h] = twice(k)
        firsts = wide(back)
        scores = jnp.where(low, dot(firsts, jnp.concatenate([v, v], axis=1), T_DIMS), 0.0)
        adjoint = dot(firsts, twice(state)) + dot(wide(scores), twice(k))
        right = jnp.concatenate([q_ref[:, lanes].astype(f32), adjoint], axis=0)
        x_s[h] = jnp.zeros_like(right)
        r_s[h] = right
        p_s[h] = right
    rr0 = tuple(jnp.sum(r_s[h] * r_s[h], -1, keepdims=True) for h in range(2))

    def step(i, rrs):
        news = []
        for h in range(2):
            rr = rrs[h]
            p = p_s[h]
            first = dot(wide(p), b_s[h])
            scores = jnp.where(low_two, first[:, 128:], 0.0)
            image = first[:, :128] + dot(wide(scores), k_s[h]) + reg_ref[h] * p
            alpha = rr / (jnp.sum(p * image, -1, keepdims=True) + epsilon)
            kept = jnp.where(i < steps_ref[0, h], alpha, 0.0)
            x_s[h] = x_s[h] + kept * p
            r = r_s[h] - alpha * image
            r_s[h] = r
            new = jnp.sum(r * r, -1, keepdims=True)
            p_s[h] = r + (new / (rr + epsilon)) * p
            news.append(new)
        return tuple(news)

    lax.fori_loop(0, jnp.maximum(steps_ref[0, 0], steps_ref[0, 1]), step, rr0)

    syms, crosses = [], []
    for h in range(2):
        lanes = slice(h * 128, (h + 1) * 128)
        k, v, back = k_ref[:, lanes], v_ref[:, lanes], back_ref[:, lanes]
        state = mats[2 + h]
        sol, dual = x_s[h, :128, :], x_s[h, 128:, :]
        sol_ref[:, lanes] = sol
        dual_ref[:, lanes] = dual
        grad_q_ref[:, lanes] = dual.astype(bf16)
        firsts = wide(sol)
        scores = jnp.where(low, dot(firsts, jnp.concatenate([k, k], axis=1), T_DIMS), 0.0)
        mixed = dot(firsts, jnp.concatenate([state, state], axis=1), T_DIMS) + dot(wide(scores), twice(v))
        mixed_ref[:, lanes] = mixed.astype(bf16)
        sol_high, sol_low = halves(sol)
        dual_high, dual_low = halves(dual)
        back_high, back_low = halves(back)
        outer = dot(
            jnp.concatenate([dual_high, dual_high, dual_low], axis=0),
            jnp.concatenate([sol_high, sol_low, sol_high], axis=0),
            L_DIMS,
        )
        syms.append(outer + outer.T)
        crosses.append(
            dot(
                jnp.concatenate([back_high, back_high, back_low], axis=0),
                jnp.concatenate([sol_high, sol_low, sol_high], axis=0),
                L_DIMS,
            )
        )
    pack(syms + crosses, send_ref)


def inner_kernel(k_ref, v_ref, back_ref, sol_ref, dual_ref, gk_ref, gv_ref):
    up = causal(128, True)
    for h in range(2):
        lanes = slice(h * 128, (h + 1) * 128)
        k, v, back = k_ref[:, lanes], v_ref[:, lanes], back_ref[:, lanes]
        sol, dual = sol_ref[:, lanes], dual_ref[:, lanes]
        kk = jnp.concatenate([k, k], axis=1)
        vv = jnp.concatenate([v, v], axis=1)
        one = wide(jnp.where(up, dot(kk, wide(sol), T_DIMS), 0.0))
        two = wide(jnp.where(up, dot(kk, wide(dual), T_DIMS), 0.0))
        three = wide(jnp.where(up, dot(vv, wide(back), T_DIMS), 0.0))
        sol_b, dual_b, back_b = sol.astype(bf16), dual.astype(bf16), back.astype(bf16)
        gk_ref[:, lanes] = dot(three, twice(sol_b)) - dot(one, twice(dual_b)) - dot(two, twice(sol_b))
        gv_ref[:, lanes] = dot(one, twice(back_b))


def final_kernel(k_ref, v_ref, gk_ref, gv_ref, suf_ref, grad_k_ref, grad_v_ref):
    sym0, sym1, cross0, cross1 = unpack(suf_ref)
    k, v = heads_apart(k_ref[...]), heads_apart(v_ref[...])
    cross = jnp.concatenate([cross0, cross1], axis=0)
    sym = jnp.concatenate([sym0, sym1], axis=0)
    cross_lanes = jnp.concatenate([cross0, cross1], axis=1)
    grad_k_ref[...] = (gk_ref[...] + dot(v, cross) - dot(k, sym)).astype(bf16)
    grad_v_ref[...] = (gv_ref[...] + dot(k, cross_lanes, T_DIMS)).astype(bf16)


def call(kernel, outs, n_smem=0, n_in=0, scratch=(), flops=0, bytes_accessed=0):
    return pl.pallas_call(
        kernel,
        out_shape=[jax.ShapeDtypeStruct(s, d) for s, d in outs],
        in_specs=[pl.BlockSpec(memory_space=pltpu.SMEM)] * n_smem
        + [pl.BlockSpec(memory_space=pltpu.VMEM)] * n_in,
        out_specs=[pl.BlockSpec(memory_space=pltpu.VMEM)] * len(outs),
        scratch_shapes=list(scratch),
        compiler_params=pltpu.CompilerParams(vmem_limit_bytes=24 * 1024 * 1024),
        cost_estimate=pl.CostEstimate(flops=flops, bytes_accessed=bytes_accessed, transcendentals=0),
    )


def local(queries, keys, values, reg, steps, w_out, d_y):
    size_c, head_count, head_size = queries.shape
    width = head_count * head_size
    spans = lax.axis_size("seq")
    packed = (spans * ROWS, head_size)
    tokens = (size_c, width)
    pairs = (size_c * head_count, head_size)
    heads = (size_c, head_count, head_size)

    def exchange(a):
        parts = a.reshape(spans, ROWS // 2, 2, head_size).transpose(0, 2, 1, 3)
        moved = lax.all_to_all(parts.reshape(spans, 2, -1), "seq", 0, 0)
        parts = moved.reshape(spans, 2, ROWS // 2, head_size).transpose(0, 2, 1, 3)
        return parts.reshape(packed)

    def scan(a, later):
        return call(functools.partial(scan_kernel, later), [(packed, bf16)], 0, 1)(a)[0]

    k_pairs, v_pairs = keys.reshape(pairs), values.reshape(pairs)
    (own,) = call(own_kernel, [(packed, bf16)], 0, 2)(k_pairs, v_pairs)
    rows = d_y.shape[0]
    dy_rows = lax.all_gather(jnp.concatenate([d_y, d_y], axis=0), "head", axis=0, tiled=True)
    back = lax.dot_general(dy_rows, w_out, T_DIMS, preferred_element_type=f32)
    back = back.reshape(-1, 2 * rows, width)[:, :rows].reshape(tokens)
    q, k, v = (a.reshape(tokens) for a in (queries, keys, values))
    pre = exchange(scan(exchange(own), False))

    sol, dual, mixed, grad_q, send = call(
        solve_kernel,
        [(tokens, f32), (tokens, f32), (tokens, bf16), (tokens, bf16), (packed, bf16)],
        2,
        5,
        [
            pltpu.VMEM((2, 256, 128), f32),
            pltpu.VMEM((2, 256, 128), f32),
            pltpu.VMEM((2, 256, 128), f32),
            pltpu.VMEM((2, 256, 256), bf16),
            pltpu.VMEM((2, 256, 128), bf16),
        ],
        flops=2 * 10**9,
    )(steps, reg, q, k, v, back, pre)
    out = lax.psum_scatter(
        jnp.dot(mixed, w_out, preferred_element_type=f32).astype(bf16),
        "head",
        scatter_dimension=0,
        tiled=True,
    )
    suf = exchange(scan(exchange(send), True))
    gk, gv = call(inner_kernel, [(tokens, f32), (tokens, f32)], 0, 5, flops=2 * 10**8)(
        k, v, back, sol, dual
    )
    grad_k, grad_v = call(final_kernel, [(pairs, bf16), (pairs, bf16)], 0, 5)(
        k_pairs, v_pairs, gk.reshape(heads).reshape(pairs), gv.reshape(heads).reshape(pairs), suf
    )
    return out, grad_q.reshape(heads), grad_k.reshape(heads), grad_v.reshape(heads)


def solution(mesh):
    placed = (
        P("seq", "head", None),
        P("seq", "head", None),
        P("seq", "head", None),
        P("head"),
        P("seq", "head"),
        P("head", None),
        P(("seq", "head"), None),
    )
    return jax.shard_map(
        local,
        mesh=mesh,
        in_specs=placed,
        out_specs=(
            P(("seq", "head"), None),
            P("seq", "head", None),
            P("seq", "head", None),
            P("seq", "head", None),
        ),
        check_vma=False,
    )
```

```python
import functools
import jax
import jax.numpy as jnp
from jax import lax
from jax.experimental import pallas as pl
from jax.experimental.pallas import tpu as pltpu
from jax.sharding import Mesh
from jax.sharding import PartitionSpec as P

STEPS_MAX = 12
SEQ = ("chip", "core")
epsilon = 1e-06
f32 = jnp.float32
bf16 = jnp.bfloat16
N_DIMS = (((1,), (0,)), ((), ()))
T_DIMS = (((1,), (1,)), ((), ()))
L_DIMS = (((0,), (0,)), ((), ()))


def dot(a, b, dims=N_DIMS):
    return lax.dot_general(a, b, dims, preferred_element_type=f32)


def halves(a):
    high = a.astype(bf16)
    return high, (a - high.astype(f32)).astype(bf16)


def wide(a):
    return jnp.concatenate(halves(a), axis=1)


def twice(b):
    return jnp.concatenate([b, b], axis=0)


def causal(rows, transposed=False):
    r = lax.rem(lax.broadcasted_iota(jnp.int32, (rows, 128), 0), 128)
    c = lax.broadcasted_iota(jnp.int32, (rows, 128), 1)
    return (r <= c) if transposed else (r >= c)


ROWS = 6
STACK = 512


def heads_apart(both):
    head = lax.rem(lax.broadcasted_iota(jnp.int32, (256, 1), 0), 2)
    first = jnp.where(head == 0, 1.0, 0.0).astype(bf16)
    return jnp.concatenate([both * first, both * (1 - first)], axis=1)


def pack(mats, out_ref):
    for i, mat in enumerate(mats):
        out_ref[i * 128 : (i + 1) * 128, :] = mat.astype(bf16)
    rest = out_ref.shape[0] - STACK
    out_ref[STACK:, :] = jnp.zeros((rest, 128), bf16)


def unpack(ref):
    return [ref[i * 128 : (i + 1) * 128, :] for i in range(4)]


def heads_apart_turned(both):
    turned = both.T
    head = lax.rem(lax.broadcasted_iota(jnp.int32, (1, 256), 1), 2)
    first = jnp.where(head == 0, 1.0, 0.0).astype(bf16)
    return jnp.concatenate([turned * first, turned * (1 - first)], axis=0)


def own_kernel(k_ref, v_ref, out_ref):
    k = k_ref[...]
    sums = dot(heads_apart_turned(k), k)
    states = dot(heads_apart_turned(v_ref[...]), k)
    pack([sums[:128], sums[128:], states[:128], states[128:]], out_ref)


def scan_kernel(later, x_ref, out_ref):
    size = 16 * ROWS
    blocks = x_ref.shape[0] // size

    def place(shape, dim):
        i = lax.broadcasted_iota(jnp.int32, shape, dim)
        span = lax.shift_right_logical(i * 10923, 16)
        return span, i - ROWS * span

    r_span, r_row = place((size, 1), 0)
    c_span, c_row = place((1, size), 1)
    same = r_row == c_row
    reach = (c_span > r_span) if later else (c_span < r_span)
    tri = jnp.where(reach & same, 1.0, 0.0)
    every = jnp.where(same, 1.0, 0.0)
    side = jnp.concatenate([x_ref[g * size : (g + 1) * size, :] for g in range(blocks)], axis=1)
    sums = dot(jnp.concatenate([tri, every], axis=0).astype(bf16), side)
    carry = None
    for g in reversed(range(blocks)) if later else range(blocks):
        lanes = slice(g * 128, (g + 1) * 128)
        inside = sums[:size, lanes]
        out_ref[g * size : (g + 1) * size, :] = (inside if carry is None else inside + carry).astype(bf16)
        total = sums[size:, lanes]
        carry = total if carry is None else carry + total


def solve_kernel(
    cfg_ref,
    q_ref,
    k_ref,
    v_ref,
    back_ref,
    pre_ref,
    sol_ref,
    dual_ref,
    mixed_ref,
    grad_q_ref,
    send_ref,
    x_s,
    r_s,
    p_s,
    b_s,
    k_s,
):
    mats = unpack(pre_ref)
    low = causal(128)
    low_two = causal(256)
    ridges = [jnp.broadcast_to(cfg_ref[:, h : h + 1], (1, 128)) for h in range(2)]
    counts = [cfg_ref[:, 2 + h : 3 + h] for h in range(2)]
    rrs = []
    for h in range(2):
        lanes = slice(h * 128, (h + 1) * 128)
        k, v, back = k_ref[:, lanes], v_ref[:, lanes], back_ref[:, lanes]
        cov, state = mats[h], mats[2 + h]
        both = jnp.concatenate([cov, k.T], axis=1)
        b_s[h] = twice(both)
        k_s[h] = twice(k)
        firsts = wide(back)
        scores = jnp.where(low, dot(firsts, jnp.concatenate([v, v], axis=1), T_DIMS), 0.0)
        adjoint = dot(firsts, twice(state)) + dot(wide(scores), twice(k))
        right = jnp.concatenate([q_ref[:, lanes].astype(f32), adjoint], axis=0)
        x_s[h] = jnp.zeros_like(right)
        r_s[h] = right
        p_s[h] = right
        rrs.append(jnp.sum(right * right, -1, keepdims=True))

    for i in range(STEPS_MAX):
        ps = [p_s[h] for h in range(2)]
        firsts = [dot(wide(ps[h]), b_s[h]) for h in range(2)]
        scores = [jnp.where(low_two, firsts[h][:, 128:], 0.0) for h in range(2)]
        seconds = [dot(wide(scores[h]), k_s[h]) for h in range(2)]
        images = [firsts[h][:, :128] + seconds[h] + ridges[h] * ps[h] for h in range(2)]
        alphas = [rrs[h] / (jnp.sum(ps[h] * images[h], -1, keepdims=True) + epsilon) for h in range(2)]
        for h in range(2):
            kept = jnp.where(i < counts[h], alphas[h], 0.0)
            x_s[h] = x_s[h] + kept * ps[h]
            if i == STEPS_MAX - 1:
                continue
            r = r_s[h] - alphas[h] * images[h]
            r_s[h] = r
            new = jnp.sum(r * r, -1, keepdims=True)
            p_s[h] = r + (new / (rrs[h] + epsilon)) * ps[h]
            rrs[h] = new

    syms, crosses = [], []
    for h in range(2):
        lanes = slice(h * 128, (h + 1) * 128)
        k, v, back = k_ref[:, lanes], v_ref[:, lanes], back_ref[:, lanes]
        state = mats[2 + h]
        sol, dual = x_s[h, :128, :], x_s[h, 128:, :]
        sol_ref[:, lanes] = sol
        dual_ref[:, lanes] = dual
        grad_q_ref[:, lanes] = dual.astype(bf16)
        firsts = wide(sol)
        scores = jnp.where(low, dot(firsts, jnp.concatenate([k, k], axis=1), T_DIMS), 0.0)
        mixed = dot(firsts, jnp.concatenate([state, state], axis=1), T_DIMS) + dot(wide(scores), twice(v))
        mixed_ref[:, lanes] = mixed.astype(bf16)
        sol_high, sol_low = halves(sol)
        dual_high, dual_low = halves(dual)
        back_high, back_low = halves(back)
        outer = dot(
            jnp.concatenate([dual_high, dual_high, dual_low], axis=0),
            jnp.concatenate([sol_high, sol_low, sol_high], axis=0),
            L_DIMS,
        )
        syms.append(outer + outer.T)
        crosses.append(
            dot(
                jnp.concatenate([back_high, back_high, back_low], axis=0),
                jnp.concatenate([sol_high, sol_low, sol_high], axis=0),
                L_DIMS,
            )
        )
    pack(syms + crosses, send_ref)


def inner_kernel(k_ref, v_ref, back_ref, sol_ref, dual_ref, gk_ref, gv_ref):
    up = causal(128, True)
    for h in range(2):
        lanes = slice(h * 128, (h + 1) * 128)
        k, v, back = k_ref[:, lanes], v_ref[:, lanes], back_ref[:, lanes]
        sol, dual = sol_ref[:, lanes], dual_ref[:, lanes]
        kk = jnp.concatenate([k, k], axis=1)
        vv = jnp.concatenate([v, v], axis=1)
        one = wide(jnp.where(up, dot(kk, wide(sol), T_DIMS), 0.0))
        two = wide(jnp.where(up, dot(kk, wide(dual), T_DIMS), 0.0))
        three = wide(jnp.where(up, dot(vv, wide(back), T_DIMS), 0.0))
        sol_b, dual_b, back_b = sol.astype(bf16), dual.astype(bf16), back.astype(bf16)
        gk_ref[:, lanes] = dot(three, twice(sol_b)) - dot(one, twice(dual_b)) - dot(two, twice(sol_b))
        gv_ref[:, lanes] = dot(one, twice(back_b))


def final_kernel(k_ref, v_ref, gk_ref, gv_ref, suf_ref, grad_k_ref, grad_v_ref):
    sym0, sym1, cross0, cross1 = unpack(suf_ref)
    k, v = heads_apart(k_ref[...]), heads_apart(v_ref[...])
    cross = jnp.concatenate([cross0, cross1], axis=0)
    sym = jnp.concatenate([sym0, sym1], axis=0)
    cross_lanes = jnp.concatenate([cross0, cross1], axis=1)
    grad_k_ref[...] = (gk_ref[...] + dot(v, cross) - dot(k, sym)).astype(bf16)
    grad_v_ref[...] = (gv_ref[...] + dot(k, cross_lanes, T_DIMS)).astype(bf16)


def call(kernel, outs, n_smem=0, n_in=0, scratch=(), flops=0, bytes_accessed=0, vmem=24):
    return pl.pallas_call(
        kernel,
        out_shape=[jax.ShapeDtypeStruct(s, d) for s, d in outs],
        in_specs=[pl.BlockSpec(memory_space=pltpu.SMEM)] * n_smem
        + [pl.BlockSpec(memory_space=pltpu.VMEM)] * n_in,
        out_specs=[pl.BlockSpec(memory_space=pltpu.VMEM)] * len(outs),
        scratch_shapes=list(scratch),
        compiler_params=pltpu.CompilerParams(vmem_limit_bytes=vmem * 1024 * 1024),
        cost_estimate=pl.CostEstimate(flops=flops, bytes_accessed=bytes_accessed, transcendentals=0),
    )


def local(queries, keys, values, reg, steps, w_out, d_y):
    size_c, head_count, head_size = queries.shape
    width = head_count * head_size
    spans = lax.axis_size(SEQ)
    packed = (spans * ROWS, head_size)
    tokens = (size_c, width)
    pairs = (size_c * head_count, head_size)
    heads = (size_c, head_count, head_size)

    def exchange(a):
        parts = a.reshape(spans, ROWS // 2, 2, head_size).transpose(0, 2, 1, 3)
        moved = lax.all_to_all(parts.reshape(spans, 2, -1), SEQ, 0, 0)
        parts = moved.reshape(spans, 2, ROWS // 2, head_size).transpose(0, 2, 1, 3)
        return parts.reshape(packed)

    def scan(a, later):
        return call(functools.partial(scan_kernel, later), [(packed, bf16)], 0, 1)(a)[0]

    k_pairs, v_pairs = keys.reshape(pairs), values.reshape(pairs)
    (own,) = call(own_kernel, [(packed, bf16)], 0, 2, vmem=56)(k_pairs, v_pairs)
    dy_rows = lax.all_gather(d_y, ("core", "head"), axis=0, tiled=True)
    dy_rows = lax.dynamic_slice_in_dim(dy_rows, lax.axis_index("core") * size_c, size_c, 0)
    back = lax.dot_general(dy_rows, w_out, T_DIMS, preferred_element_type=f32)
    q, k, v = (a.reshape(tokens) for a in (queries, keys, values))
    cfg = jnp.concatenate([reg, steps[0].astype(f32)]).reshape(1, -1)
    pre = exchange(scan(exchange(own), False))

    sol, dual, mixed, grad_q, send = call(
        solve_kernel,
        [(tokens, f32), (tokens, f32), (tokens, bf16), (tokens, bf16), (packed, bf16)],
        0,
        6,
        [
            pltpu.VMEM((2, 256, 128), f32),
            pltpu.VMEM((2, 256, 128), f32),
            pltpu.VMEM((2, 256, 128), f32),
            pltpu.VMEM((2, 256, 256), bf16),
            pltpu.VMEM((2, 256, 128), bf16),
        ],
        flops=2 * 10**9,
    )(cfg, q, k, v, back, pre)
    out = lax.psum_scatter(
        jnp.dot(mixed, w_out, preferred_element_type=f32).astype(bf16),
        "head",
        scatter_dimension=0,
        tiled=True,
    )
    suf = exchange(scan(exchange(send), True))
    gk, gv = call(inner_kernel, [(tokens, f32), (tokens, f32)], 0, 5, flops=2 * 10**8)(
        k, v, back, sol, dual
    )
    grad_k, grad_v = call(final_kernel, [(pairs, bf16), (pairs, bf16)], 0, 5)(
        k_pairs, v_pairs, gk.reshape(heads).reshape(pairs), gv.reshape(heads).reshape(pairs), suf
    )
    return out, grad_q.reshape(heads), grad_k.reshape(heads), grad_v.reshape(heads)


def solution(mesh):
    spans, groups = mesh.devices.shape
    apart = Mesh(mesh.devices.reshape(spans // 2, 2, groups), SEQ + ("head",))
    placed = (
        P(SEQ, "head", None),
        P(SEQ, "head", None),
        P(SEQ, "head", None),
        P("head"),
        P(SEQ, "head"),
        P("head", None),
        P(SEQ + ("head",), None),
    )
    return jax.shard_map(
        local,
        mesh=apart,
        in_specs=placed,
        out_specs=(
            P(SEQ + ("head",), None),
            P(SEQ, "head", None),
            P(SEQ, "head", None),
            P(SEQ, "head", None),
        ),
        check_vma=False,
    )
```

```python
import functools
import jax
import jax.numpy as jnp
from jax import lax
from jax.experimental import pallas as pl
from jax.experimental.pallas import tpu as pltpu
from jax.sharding import Mesh
from jax.sharding import PartitionSpec as P

STEPS_MAX = 12
SEQ = ("chip", "core")
epsilon = 1e-06
f32 = jnp.float32
bf16 = jnp.bfloat16
N_DIMS = (((1,), (0,)), ((), ()))
T_DIMS = (((1,), (1,)), ((), ()))
L_DIMS = (((0,), (0,)), ((), ()))


def dot(a, b, dims=N_DIMS):
    return lax.dot_general(a, b, dims, preferred_element_type=f32)


def halves(a):
    high = a.astype(bf16)
    return high, (a - high.astype(f32)).astype(bf16)


def wide(a):
    return jnp.concatenate(halves(a), axis=1)


def twice(b):
    return jnp.concatenate([b, b], axis=0)


def causal(rows, transposed=False):
    r = lax.rem(lax.broadcasted_iota(jnp.int32, (rows, 128), 0), 128)
    c = lax.broadcasted_iota(jnp.int32, (rows, 128), 1)
    return (r <= c) if transposed else (r >= c)


ROWS = 6
STACK = 512


def heads_apart(both):
    head = lax.rem(lax.broadcasted_iota(jnp.int32, (256, 1), 0), 2)
    first = jnp.where(head == 0, 1.0, 0.0).astype(bf16)
    return jnp.concatenate([both * first, both * (1 - first)], axis=1)


def pack(mats, out_ref):
    for i, mat in enumerate(mats):
        out_ref[i * 128 : (i + 1) * 128, :] = mat.astype(bf16)
    rest = out_ref.shape[0] - STACK
    out_ref[STACK:, :] = jnp.zeros((rest, 128), bf16)


def unpack(ref):
    return [ref[i * 128 : (i + 1) * 128, :] for i in range(4)]


def heads_apart_turned(both):
    turned = both.T
    head = lax.rem(lax.broadcasted_iota(jnp.int32, (1, 256), 1), 2)
    first = jnp.where(head == 0, 1.0, 0.0).astype(bf16)
    return jnp.concatenate([turned * first, turned * (1 - first)], axis=0)


def own_kernel(k_ref, v_ref, out_ref):
    k = k_ref[...]
    sums = dot(heads_apart_turned(k), k)
    states = dot(heads_apart_turned(v_ref[...]), k)
    pack([sums[:128], sums[128:], states[:128], states[128:]], out_ref)


def scan_kernel(later, x_ref, out_ref):
    size = 16 * ROWS
    blocks = x_ref.shape[0] // size

    def place(shape, dim):
        i = lax.broadcasted_iota(jnp.int32, shape, dim)
        span = lax.shift_right_logical(i * 10923, 16)
        return span, i - ROWS * span

    r_span, r_row = place((size, 1), 0)
    c_span, c_row = place((1, size), 1)
    same = r_row == c_row
    reach = (c_span > r_span) if later else (c_span < r_span)
    tri = jnp.where(reach & same, 1.0, 0.0)
    every = jnp.where(same, 1.0, 0.0)
    side = jnp.concatenate([x_ref[g * size : (g + 1) * size, :] for g in range(blocks)], axis=1)
    sums = dot(jnp.concatenate([tri, every], axis=0).astype(bf16), side)
    carry = None
    for g in reversed(range(blocks)) if later else range(blocks):
        lanes = slice(g * 128, (g + 1) * 128)
        inside = sums[:size, lanes]
        out_ref[g * size : (g + 1) * size, :] = (inside if carry is None else inside + carry).astype(bf16)
        total = sums[size:, lanes]
        carry = total if carry is None else carry + total


def solve_kernel(
    cfg_ref,
    q_ref,
    k_ref,
    v_ref,
    back_ref,
    pre_ref,
    sol_ref,
    dual_ref,
    mixed_ref,
    grad_q_ref,
    send_ref,
    x_s,
    r_s,
    p_s,
    b_s,
    k_s,
):
    mats = unpack(pre_ref)
    low = causal(128)
    low_two = causal(256)
    ridges = [jnp.broadcast_to(cfg_ref[:, h : h + 1], (1, 128)) for h in range(2)]
    counts = [jnp.broadcast_to(cfg_ref[:, 2 + h : 3 + h], (1, 128)) for h in range(2)]
    rrs = []
    for h in range(2):
        lanes = slice(h * 128, (h + 1) * 128)
        k, v, back = k_ref[:, lanes], v_ref[:, lanes], back_ref[:, lanes]
        cov, state = mats[h], mats[2 + h]
        both = jnp.concatenate([cov, k.T], axis=1)
        b_s[h] = twice(both)
        k_s[h] = twice(k)
        firsts = wide(back)
        scores = jnp.where(low, dot(firsts, jnp.concatenate([v, v], axis=1), T_DIMS), 0.0)
        adjoint = dot(firsts, twice(state)) + dot(wide(scores), twice(k))
        right = jnp.concatenate([q_ref[:, lanes].astype(f32), adjoint], axis=0)
        x_s[h] = jnp.zeros_like(right)
        r_s[h] = right
        p_s[h] = right
        rrs.append(jnp.sum(right * right, -1, keepdims=True))

    for i in range(STEPS_MAX):
        ps = [p_s[h] for h in range(2)]
        firsts = [dot(wide(ps[h]), b_s[h]) for h in range(2)]
        scores = [jnp.where(low_two, firsts[h][:, 128:], 0.0) for h in range(2)]
        seconds = [dot(wide(scores[h]), k_s[h]) for h in range(2)]
        images = [firsts[h][:, :128] + seconds[h] + ridges[h] * ps[h] for h in range(2)]
        alphas = [rrs[h] / (jnp.sum(ps[h] * images[h], -1, keepdims=True) + epsilon) for h in range(2)]
        for h in range(2):
            live = jnp.where(i < counts[h], 1.0, 0.0)
            x_s[h] = x_s[h] + alphas[h] * (ps[h] * live)
            if i == STEPS_MAX - 1:
                continue
            r = r_s[h] - alphas[h] * images[h]
            r_s[h] = r
            new = jnp.sum(r * r, -1, keepdims=True)
            p_s[h] = r + (new / (rrs[h] + epsilon)) * ps[h]
            rrs[h] = new

    syms, crosses = [], []
    for h in range(2):
        lanes = slice(h * 128, (h + 1) * 128)
        k, v, back = k_ref[:, lanes], v_ref[:, lanes], back_ref[:, lanes]
        state = mats[2 + h]
        sol, dual = x_s[h, :128, :], x_s[h, 128:, :]
        sol_ref[:, lanes] = sol
        dual_ref[:, lanes] = dual
        grad_q_ref[:, lanes] = dual.astype(bf16)
        firsts = wide(sol)
        scores = jnp.where(low, dot(firsts, jnp.concatenate([k, k], axis=1), T_DIMS), 0.0)
        mixed = dot(firsts, jnp.concatenate([state, state], axis=1), T_DIMS) + dot(wide(scores), twice(v))
        mixed_ref[:, lanes] = mixed.astype(bf16)
        sol_high, sol_low = halves(sol)
        dual_high, dual_low = halves(dual)
        back_high, back_low = halves(back)
        outer = dot(
            jnp.concatenate([dual_high, dual_high, dual_low], axis=0),
            jnp.concatenate([sol_high, sol_low, sol_high], axis=0),
            L_DIMS,
        )
        syms.append(outer + outer.T)
        crosses.append(
            dot(
                jnp.concatenate([back_high, back_high, back_low], axis=0),
                jnp.concatenate([sol_high, sol_low, sol_high], axis=0),
                L_DIMS,
            )
        )
    pack(syms + crosses, send_ref)


def inner_kernel(k_ref, v_ref, back_ref, sol_ref, dual_ref, gk_ref, gv_ref):
    up = causal(128, True)
    for h in range(2):
        lanes = slice(h * 128, (h + 1) * 128)
        k, v, back = k_ref[:, lanes], v_ref[:, lanes], back_ref[:, lanes]
        sol, dual = sol_ref[:, lanes], dual_ref[:, lanes]
        kk = jnp.concatenate([k, k], axis=1)
        vv = jnp.concatenate([v, v], axis=1)
        one = wide(jnp.where(up, dot(kk, wide(sol), T_DIMS), 0.0))
        two = wide(jnp.where(up, dot(kk, wide(dual), T_DIMS), 0.0))
        three = wide(jnp.where(up, dot(vv, wide(back), T_DIMS), 0.0))
        sol_b, dual_b, back_b = sol.astype(bf16), dual.astype(bf16), back.astype(bf16)
        gk_ref[:, lanes] = dot(three, twice(sol_b)) - dot(one, twice(dual_b)) - dot(two, twice(sol_b))
        gv_ref[:, lanes] = dot(one, twice(back_b))


def final_kernel(k_ref, v_ref, gk_ref, gv_ref, suf_ref, grad_k_ref, grad_v_ref):
    sym0, sym1, cross0, cross1 = unpack(suf_ref)
    k, v = heads_apart(k_ref[...]), heads_apart(v_ref[...])
    cross = jnp.concatenate([cross0, cross1], axis=0)
    sym = jnp.concatenate([sym0, sym1], axis=0)
    cross_lanes = jnp.concatenate([cross0, cross1], axis=1)
    grad_k_ref[...] = (gk_ref[...] + dot(v, cross) - dot(k, sym)).astype(bf16)
    grad_v_ref[...] = (gv_ref[...] + dot(k, cross_lanes, T_DIMS)).astype(bf16)


def call(kernel, outs, n_smem=0, n_in=0, scratch=(), flops=0, bytes_accessed=0, vmem=24):
    return pl.pallas_call(
        kernel,
        out_shape=[jax.ShapeDtypeStruct(s, d) for s, d in outs],
        in_specs=[pl.BlockSpec(memory_space=pltpu.SMEM)] * n_smem
        + [pl.BlockSpec(memory_space=pltpu.VMEM)] * n_in,
        out_specs=[pl.BlockSpec(memory_space=pltpu.VMEM)] * len(outs),
        scratch_shapes=list(scratch),
        compiler_params=pltpu.CompilerParams(vmem_limit_bytes=vmem * 1024 * 1024),
        cost_estimate=pl.CostEstimate(flops=flops, bytes_accessed=bytes_accessed, transcendentals=0),
    )


def local(queries, keys, values, reg, steps, w_out, d_y):
    size_c, head_count, head_size = queries.shape
    width = head_count * head_size
    spans = lax.axis_size(SEQ)
    packed = (spans * ROWS, head_size)
    tokens = (size_c, width)
    pairs = (size_c * head_count, head_size)
    heads = (size_c, head_count, head_size)

    def exchange(a):
        parts = a.reshape(spans, ROWS // 2, 2, head_size).transpose(0, 2, 1, 3)
        moved = lax.all_to_all(parts.reshape(spans, 2, -1), SEQ, 0, 0)
        parts = moved.reshape(spans, 2, ROWS // 2, head_size).transpose(0, 2, 1, 3)
        return parts.reshape(packed)

    def scan(a, later):
        return call(functools.partial(scan_kernel, later), [(packed, bf16)], 0, 1)(a)[0]

    k_pairs, v_pairs = keys.reshape(pairs), values.reshape(pairs)
    (own,) = call(own_kernel, [(packed, bf16)], 0, 2, vmem=56)(k_pairs, v_pairs)
    dy_rows = lax.all_gather(d_y, ("core", "head"), axis=0, tiled=True)
    dy_rows = lax.dynamic_slice_in_dim(dy_rows, lax.axis_index("core") * size_c, size_c, 0)
    back = lax.dot_general(dy_rows, w_out, T_DIMS, preferred_element_type=f32)
    q, k, v = (a.reshape(tokens) for a in (queries, keys, values))
    cfg = jnp.concatenate([reg, steps[0].astype(f32)]).reshape(1, -1)
    pre = exchange(scan(exchange(own), False))

    sol, dual, mixed, grad_q, send = call(
        solve_kernel,
        [(tokens, f32), (tokens, f32), (tokens, bf16), (tokens, bf16), (packed, bf16)],
        0,
        6,
        [
            pltpu.VMEM((2, 256, 128), f32),
            pltpu.VMEM((2, 256, 128), f32),
            pltpu.VMEM((2, 256, 128), f32),
            pltpu.VMEM((2, 256, 256), bf16),
            pltpu.VMEM((2, 256, 128), bf16),
        ],
        flops=2 * 10**9,
    )(cfg, q, k, v, back, pre)
    out = lax.psum_scatter(
        jnp.dot(mixed, w_out, preferred_element_type=f32).astype(bf16),
        "head",
        scatter_dimension=0,
        tiled=True,
    )
    suf = exchange(scan(exchange(send), True))
    gk, gv = call(inner_kernel, [(tokens, f32), (tokens, f32)], 0, 5, flops=2 * 10**8)(
        k, v, back, sol, dual
    )
    grad_k, grad_v = call(final_kernel, [(pairs, bf16), (pairs, bf16)], 0, 5)(
        k_pairs, v_pairs, gk.reshape(heads).reshape(pairs), gv.reshape(heads).reshape(pairs), suf
    )
    return out, grad_q.reshape(heads), grad_k.reshape(heads), grad_v.reshape(heads)


def solution(mesh):
    spans, groups = mesh.devices.shape
    apart = Mesh(mesh.devices.reshape(spans // 2, 2, groups), SEQ + ("head",))
    placed = (
        P(SEQ, "head", None),
        P(SEQ, "head", None),
        P(SEQ, "head", None),
        P("head"),
        P(SEQ, "head"),
        P("head", None),
        P(SEQ + ("head",), None),
    )
    return jax.shard_map(
        local,
        mesh=apart,
        in_specs=placed,
        out_specs=(
            P(SEQ + ("head",), None),
            P(SEQ, "head", None),
            P(SEQ, "head", None),
            P(SEQ, "head", None),
        ),
        check_vma=False,
    )
```

```python
import functools
import jax
import jax.numpy as jnp
from jax import lax
from jax.experimental import pallas as pl
from jax.experimental.pallas import tpu as pltpu
from jax.sharding import Mesh
from jax.sharding import PartitionSpec as P

STEPS_MAX = 12
SEQ = ("chip", "core")
epsilon = 1e-06
f32 = jnp.float32
bf16 = jnp.bfloat16
N_DIMS = (((1,), (0,)), ((), ()))
T_DIMS = (((1,), (1,)), ((), ()))
L_DIMS = (((0,), (0,)), ((), ()))


def dot(a, b, dims=N_DIMS):
    return lax.dot_general(a, b, dims, preferred_element_type=f32)


def halves(a):
    high = a.astype(bf16)
    return high, (a - high.astype(f32)).astype(bf16)


def wide(a):
    return jnp.concatenate(halves(a), axis=1)


def twice(b):
    return jnp.concatenate([b, b], axis=0)


def causal(rows, transposed=False):
    r = lax.rem(lax.broadcasted_iota(jnp.int32, (rows, 128), 0), 128)
    c = lax.broadcasted_iota(jnp.int32, (rows, 128), 1)
    return (r <= c) if transposed else (r >= c)


ROWS = 6
STACK = 512


def heads_apart(both):
    head = lax.rem(lax.broadcasted_iota(jnp.int32, (256, 1), 0), 2)
    first = jnp.where(head == 0, 1.0, 0.0).astype(bf16)
    return jnp.concatenate([both * first, both * (1 - first)], axis=1)


def pack(mats, out_ref):
    for i, mat in enumerate(mats):
        out_ref[i * 128 : (i + 1) * 128, :] = mat.astype(bf16)
    rest = out_ref.shape[0] - STACK
    out_ref[STACK:, :] = jnp.zeros((rest, 128), bf16)


def unpack(ref):
    return [ref[i * 128 : (i + 1) * 128, :] for i in range(4)]


def heads_apart_turned(both):
    turned = both.T
    head = lax.rem(lax.broadcasted_iota(jnp.int32, (1, 256), 1), 2)
    first = jnp.where(head == 0, 1.0, 0.0).astype(bf16)
    return jnp.concatenate([turned * first, turned * (1 - first)], axis=0)


def own_kernel(k_ref, v_ref, out_ref):
    k = k_ref[...]
    sums = dot(heads_apart_turned(k), k)
    states = dot(heads_apart_turned(v_ref[...]), k)
    pack([sums[:128], sums[128:], states[:128], states[128:]], out_ref)


def scan_kernel(later, x_ref, out_ref):
    size = 16 * ROWS
    blocks = x_ref.shape[0] // size

    def place(shape, dim):
        i = lax.broadcasted_iota(jnp.int32, shape, dim)
        span = lax.shift_right_logical(i * 10923, 16)
        return span, i - ROWS * span

    r_span, r_row = place((size, 1), 0)
    c_span, c_row = place((1, size), 1)
    same = r_row == c_row
    reach = (c_span > r_span) if later else (c_span < r_span)
    tri = jnp.where(reach & same, 1.0, 0.0)
    every = jnp.where(same, 1.0, 0.0)
    side = jnp.concatenate([x_ref[g * size : (g + 1) * size, :] for g in range(blocks)], axis=1)
    sums = dot(jnp.concatenate([tri, every], axis=0).astype(bf16), side)
    carry = None
    for g in reversed(range(blocks)) if later else range(blocks):
        lanes = slice(g * 128, (g + 1) * 128)
        inside = sums[:size, lanes]
        out_ref[g * size : (g + 1) * size, :] = (inside if carry is None else inside + carry).astype(bf16)
        total = sums[size:, lanes]
        carry = total if carry is None else carry + total


def solve_kernel(
    cfg_ref,
    q_ref,
    k_ref,
    v_ref,
    back_ref,
    pre_ref,
    w_ref,
    sol_ref,
    dual_ref,
    part_ref,
    send_ref,
    x_s,
    r_s,
    p_s,
    b_s,
    k_s,
):
    mats = unpack(pre_ref)
    low = causal(128)
    low_two = causal(256)
    ridges = [jnp.broadcast_to(cfg_ref[:, h : h + 1], (1, 128)) for h in range(2)]
    counts = [jnp.broadcast_to(cfg_ref[:, 2 + h : 3 + h], (1, 128)) for h in range(2)]
    rrs = []
    for h in range(2):
        lanes = slice(h * 128, (h + 1) * 128)
        k, v, back = k_ref[:, lanes], v_ref[:, lanes], back_ref[:, lanes]
        cov, state = mats[h], mats[2 + h]
        both = jnp.concatenate([cov, k.T], axis=1)
        b_s[h] = twice(both)
        k_s[h] = twice(k)
        firsts = wide(back)
        scores = jnp.where(low, dot(firsts, jnp.concatenate([v, v], axis=1), T_DIMS), 0.0)
        adjoint = dot(firsts, twice(state)) + dot(wide(scores), twice(k))
        right = jnp.concatenate([q_ref[:, lanes].astype(f32), adjoint], axis=0)
        x_s[h] = jnp.zeros_like(right)
        r_s[h] = right
        p_s[h] = right
        rrs.append(jnp.sum(right * right, -1, keepdims=True))

    for i in range(STEPS_MAX):
        ps = [p_s[h] for h in range(2)]
        firsts = [dot(wide(ps[h]), b_s[h]) for h in range(2)]
        scores = [jnp.where(low_two, firsts[h][:, 128:], 0.0) for h in range(2)]
        seconds = [dot(wide(scores[h]), k_s[h]) for h in range(2)]
        images = [firsts[h][:, :128] + seconds[h] + ridges[h] * ps[h] for h in range(2)]
        alphas = [rrs[h] / (jnp.sum(ps[h] * images[h], -1, keepdims=True) + epsilon) for h in range(2)]
        for h in range(2):
            live = jnp.where(i < counts[h], 1.0, 0.0)
            x_s[h] = x_s[h] + alphas[h] * (ps[h] * live)
            if i == STEPS_MAX - 1:
                continue
            r = r_s[h] - alphas[h] * images[h]
            r_s[h] = r
            new = jnp.sum(r * r, -1, keepdims=True)
            p_s[h] = r + (new / (rrs[h] + epsilon)) * ps[h]
            rrs[h] = new

    syms, crosses, mixes = [], [], []
    for h in range(2):
        lanes = slice(h * 128, (h + 1) * 128)
        k, v, back = k_ref[:, lanes], v_ref[:, lanes], back_ref[:, lanes]
        state = mats[2 + h]
        sol, dual = x_s[h, :128, :], x_s[h, 128:, :]
        sol_ref[:, lanes] = sol
        dual_ref[:, lanes] = dual
        firsts = wide(sol)
        scores = jnp.where(low, dot(firsts, jnp.concatenate([k, k], axis=1), T_DIMS), 0.0)
        mixed = dot(firsts, jnp.concatenate([state, state], axis=1), T_DIMS) + dot(wide(scores), twice(v))
        mixes.append(mixed.astype(bf16))
        sol_high, sol_low = halves(sol)
        dual_high, dual_low = halves(dual)
        back_high, back_low = halves(back)
        outer = dot(
            jnp.concatenate([dual_high, dual_high, dual_low], axis=0),
            jnp.concatenate([sol_high, sol_low, sol_high], axis=0),
            L_DIMS,
        )
        syms.append(outer + outer.T)
        crosses.append(
            dot(
                jnp.concatenate([back_high, back_high, back_low], axis=0),
                jnp.concatenate([sol_high, sol_low, sol_high], axis=0),
                L_DIMS,
            )
        )
    pack(syms + crosses, send_ref)
    mixes = jnp.concatenate(mixes, axis=1)
    for g in range(w_ref.shape[1] // 256):
        lanes = slice(g * 256, (g + 1) * 256)
        part_ref[:, lanes] = dot(mixes, w_ref[:, lanes]).astype(bf16)


def alternate(both):
    r = lax.broadcasted_iota(jnp.int32, (256, 256), 0)
    c = lax.broadcasted_iota(jnp.int32, (256, 256), 1)
    source = (r & 1) * 128 + lax.shift_right_logical(r, 1)
    return dot(jnp.where(c == source, 1.0, 0.0).astype(bf16), both).astype(bf16)


def final_kernel(
    k_ref, v_ref, back_ref, sol_ref, dual_ref, suf_ref, grad_q_ref, grad_k_ref, grad_v_ref
):
    mats = unpack(suf_ref)
    up = causal(128, True)
    grads = []
    for h in range(2):
        lanes = slice(h * 128, (h + 1) * 128)
        k, v, back = k_ref[:, lanes], v_ref[:, lanes], back_ref[:, lanes]
        sol, dual = sol_ref[:, lanes], dual_ref[:, lanes]
        sym, cross = mats[h], mats[2 + h]
        kk = jnp.concatenate([k, k], axis=1)
        vv = jnp.concatenate([v, v], axis=1)
        one = wide(jnp.where(up, dot(kk, wide(sol), T_DIMS), 0.0))
        two = wide(jnp.where(up, dot(kk, wide(dual), T_DIMS), 0.0))
        three = wide(jnp.where(up, dot(vv, wide(back), T_DIMS), 0.0))
        sol_b, dual_b, back_b = sol.astype(bf16), dual.astype(bf16), back.astype(bf16)
        grad_k = dot(three, twice(sol_b)) - dot(one, twice(dual_b)) - dot(two, twice(sol_b))
        grad_k = grad_k + dot(v, cross) - dot(k, sym)
        grad_v = dot(one, twice(back_b)) + dot(k, cross, T_DIMS)
        grads.append(jnp.concatenate([dual_b, grad_k.astype(bf16), grad_v.astype(bf16)], axis=1))
    both = alternate(jnp.concatenate(grads, axis=0))
    grad_q_ref[...] = both[:, :128]
    grad_k_ref[...] = both[:, 128:256]
    grad_v_ref[...] = both[:, 256:]


def call(kernel, outs, n_smem=0, n_in=0, scratch=(), flops=0, bytes_accessed=0, vmem=24):
    return pl.pallas_call(
        kernel,
        out_shape=[jax.ShapeDtypeStruct(s, d) for s, d in outs],
        in_specs=[pl.BlockSpec(memory_space=pltpu.SMEM)] * n_smem
        + [pl.BlockSpec(memory_space=pltpu.VMEM)] * n_in,
        out_specs=[pl.BlockSpec(memory_space=pltpu.VMEM)] * len(outs),
        scratch_shapes=list(scratch),
        compiler_params=pltpu.CompilerParams(vmem_limit_bytes=vmem * 1024 * 1024),
        cost_estimate=pl.CostEstimate(flops=flops, bytes_accessed=bytes_accessed, transcendentals=0),
    )


def local(queries, keys, values, reg, steps, w_out, d_y):
    size_c, head_count, head_size = queries.shape
    width = head_count * head_size
    spans = lax.axis_size(SEQ)
    packed = (spans * ROWS, head_size)
    tokens = (size_c, width)
    pairs = (size_c * head_count, head_size)
    heads = (size_c, head_count, head_size)

    def exchange(a):
        parts = a.reshape(spans, ROWS // 2, 2, head_size).transpose(0, 2, 1, 3)
        moved = lax.all_to_all(parts.reshape(spans, 2, -1), SEQ, 0, 0)
        parts = moved.reshape(spans, 2, ROWS // 2, head_size).transpose(0, 2, 1, 3)
        return parts.reshape(packed)

    def scan(a, later):
        return call(functools.partial(scan_kernel, later), [(packed, bf16)], 0, 1)(a)[0]

    k_pairs, v_pairs = keys.reshape(pairs), values.reshape(pairs)
    (own,) = call(own_kernel, [(packed, bf16)], 0, 2, vmem=56)(k_pairs, v_pairs)
    dy_rows = lax.all_gather(d_y, ("core", "head"), axis=0, tiled=True)
    dy_rows = lax.dynamic_slice_in_dim(dy_rows, lax.axis_index("core") * size_c, size_c, 0)
    back = lax.dot_general(dy_rows, w_out, T_DIMS, preferred_element_type=f32)
    q, k, v = (a.reshape(tokens) for a in (queries, keys, values))
    cfg = jnp.concatenate([reg, steps[0].astype(f32)]).reshape(1, -1)
    pre = exchange(scan(exchange(own), False))

    sol, dual, part, send = call(
        solve_kernel,
        [(tokens, f32), (tokens, f32), ((size_c, w_out.shape[1]), bf16), (packed, bf16)],
        0,
        7,
        [
            pltpu.VMEM((2, 256, 128), f32),
            pltpu.VMEM((2, 256, 128), f32),
            pltpu.VMEM((2, 256, 128), f32),
            pltpu.VMEM((2, 256, 256), bf16),
            pltpu.VMEM((2, 256, 128), bf16),
        ],
        flops=2 * 10**9,
    )(cfg, q, k, v, back, pre, w_out)
    out = lax.psum_scatter(part, "head", scatter_dimension=0, tiled=True)
    suf = exchange(scan(exchange(send), True))
    grad_q, grad_k, grad_v = call(final_kernel, [(pairs, bf16)] * 3, 0, 6)(
        k, v, back, sol, dual, suf
    )
    return out, grad_q.reshape(heads), grad_k.reshape(heads), grad_v.reshape(heads)


def solution(mesh):
    spans, groups = mesh.devices.shape
    apart = Mesh(mesh.devices.reshape(spans // 2, 2, groups), SEQ + ("head",))
    placed = (
        P(SEQ, "head", None),
        P(SEQ, "head", None),
        P(SEQ, "head", None),
        P("head"),
        P(SEQ, "head"),
        P("head", None),
        P(SEQ + ("head",), None),
    )
    return jax.shard_map(
        local,
        mesh=apart,
        in_specs=placed,
        out_specs=(
            P(SEQ + ("head",), None),
            P(SEQ, "head", None),
            P(SEQ, "head", None),
            P(SEQ, "head", None),
        ),
        check_vma=False,
    )
```

```python
import functools
import jax
import jax.numpy as jnp
from jax import lax
from jax.experimental import pallas as pl
from jax.experimental.pallas import tpu as pltpu
from jax.sharding import Mesh
from jax.sharding import PartitionSpec as P

STEPS_MAX = 12
SEQ = ("chip", "core")
epsilon = 1e-06
f32 = jnp.float32
bf16 = jnp.bfloat16
N_DIMS = (((1,), (0,)), ((), ()))
T_DIMS = (((1,), (1,)), ((), ()))
L_DIMS = (((0,), (0,)), ((), ()))


def dot(a, b, dims=N_DIMS):
    return lax.dot_general(a, b, dims, preferred_element_type=f32)


def halves(a):
    high = a.astype(bf16)
    return high, (a - high.astype(f32)).astype(bf16)


def wide(a):
    return jnp.concatenate(halves(a), axis=1)


def twice(b):
    return jnp.concatenate([b, b], axis=0)


def causal(rows, transposed=False):
    r = lax.rem(lax.broadcasted_iota(jnp.int32, (rows, 128), 0), 128)
    c = lax.broadcasted_iota(jnp.int32, (rows, 128), 1)
    return (r <= c) if transposed else (r >= c)


ROWS = 6
STACK = 512


def heads_apart(both):
    head = lax.rem(lax.broadcasted_iota(jnp.int32, (256, 1), 0), 2)
    first = jnp.where(head == 0, 1.0, 0.0).astype(bf16)
    return jnp.concatenate([both * first, both * (1 - first)], axis=1)


def pack(mats, out_ref):
    for i, mat in enumerate(mats):
        out_ref[i * 128 : (i + 1) * 128, :] = mat.astype(bf16)
    rest = out_ref.shape[0] - STACK
    out_ref[STACK:, :] = jnp.zeros((rest, 128), bf16)


def unpack(ref):
    return [ref[i * 128 : (i + 1) * 128, :] for i in range(4)]


def heads_apart_turned(both):
    turned = both.T
    head = lax.rem(lax.broadcasted_iota(jnp.int32, (1, 256), 1), 2)
    first = jnp.where(head == 0, 1.0, 0.0).astype(bf16)
    return jnp.concatenate([turned * first, turned * (1 - first)], axis=0)


def own_kernel(k_ref, v_ref, out_ref):
    k = k_ref[...]
    sums = dot(heads_apart_turned(k), k)
    states = dot(heads_apart_turned(v_ref[...]), k)
    pack([sums[:128], sums[128:], states[:128], states[128:]], out_ref)


def scan_kernel(later, x_ref, out_ref):
    size = 16 * ROWS
    blocks = x_ref.shape[0] // size

    def place(shape, dim):
        i = lax.broadcasted_iota(jnp.int32, shape, dim)
        span = lax.shift_right_logical(i * 10923, 16)
        return span, i - ROWS * span

    r_span, r_row = place((size, 1), 0)
    c_span, c_row = place((1, size), 1)
    same = r_row == c_row
    reach = (c_span > r_span) if later else (c_span < r_span)
    tri = jnp.where(reach & same, 1.0, 0.0)
    every = jnp.where(same, 1.0, 0.0)
    side = jnp.concatenate([x_ref[g * size : (g + 1) * size, :] for g in range(blocks)], axis=1)
    sums = dot(jnp.concatenate([tri, every], axis=0).astype(bf16), side)
    carry = None
    for g in reversed(range(blocks)) if later else range(blocks):
        lanes = slice(g * 128, (g + 1) * 128)
        inside = sums[:size, lanes]
        out_ref[g * size : (g + 1) * size, :] = (inside if carry is None else inside + carry).astype(bf16)
        total = sums[size:, lanes]
        carry = total if carry is None else carry + total


def solve_kernel(
    cfg_ref,
    q_ref,
    k_ref,
    v_ref,
    rows_ref,
    pre_ref,
    w_ref,
    sol_ref,
    dual_ref,
    part_ref,
    send_ref,
    back_ref,
    x_s,
    r_s,
    p_s,
    b_s,
    k_s,
    rows_s,
    w_s,
    sem,
):
    size = rows_s.shape[0]
    first_row = pl.multiple_of(lax.axis_index("core") * size, size)
    fetch = pltpu.make_async_copy(rows_ref.at[pl.ds(first_row, size), :], rows_s, sem.at[0])
    fetch_w = pltpu.make_async_copy(w_ref, w_s, sem.at[1])
    fetch.start()
    fetch_w.start()
    mats = unpack(pre_ref)
    low = causal(128)
    low_two = causal(256)
    ridges = [jnp.broadcast_to(cfg_ref[:, h : h + 1], (1, 128)) for h in range(2)]
    counts = [jnp.broadcast_to(cfg_ref[:, 2 + h : 3 + h], (1, 128)) for h in range(2)]
    for h in range(2):
        k = k_ref[:, h * 128 : (h + 1) * 128]
        b_s[h] = twice(jnp.concatenate([mats[h], k.T], axis=1))
        k_s[h] = twice(k)
    fetch.wait()
    fetch_w.wait()
    back_ref[...] = dot(rows_s[...], w_s[...], T_DIMS)
    rrs = []
    for h in range(2):
        lanes = slice(h * 128, (h + 1) * 128)
        k, v, back = k_ref[:, lanes], v_ref[:, lanes], back_ref[:, lanes]
        firsts = wide(back)
        scores = jnp.where(low, dot(firsts, jnp.concatenate([v, v], axis=1), T_DIMS), 0.0)
        adjoint = dot(firsts, twice(mats[2 + h])) + dot(wide(scores), twice(k))
        right = jnp.concatenate([q_ref[:, lanes].astype(f32), adjoint], axis=0)
        x_s[h] = jnp.zeros_like(right)
        r_s[h] = right
        p_s[h] = right
        rrs.append(jnp.sum(right * right, -1, keepdims=True))

    for i in range(STEPS_MAX):
        ps = [p_s[h] for h in range(2)]
        firsts = [dot(wide(ps[h]), b_s[h]) for h in range(2)]
        scores = [jnp.where(low_two, firsts[h][:, 128:], 0.0) for h in range(2)]
        seconds = [dot(wide(scores[h]), k_s[h]) for h in range(2)]
        images = [firsts[h][:, :128] + seconds[h] + ridges[h] * ps[h] for h in range(2)]
        alphas = [rrs[h] / (jnp.sum(ps[h] * images[h], -1, keepdims=True) + epsilon) for h in range(2)]
        for h in range(2):
            live = jnp.where(i < counts[h], 1.0, 0.0)
            x_s[h] = x_s[h] + alphas[h] * (ps[h] * live)
            if i == STEPS_MAX - 1:
                continue
            r = r_s[h] - alphas[h] * images[h]
            r_s[h] = r
            new = jnp.sum(r * r, -1, keepdims=True)
            p_s[h] = r + (new / (rrs[h] + epsilon)) * ps[h]
            rrs[h] = new

    syms, crosses, mixes = [], [], []
    for h in range(2):
        lanes = slice(h * 128, (h + 1) * 128)
        k, v, back = k_ref[:, lanes], v_ref[:, lanes], back_ref[:, lanes]
        state = mats[2 + h]
        sol, dual = x_s[h, :128, :], x_s[h, 128:, :]
        sol_ref[:, lanes] = sol
        dual_ref[:, lanes] = dual
        firsts = wide(sol)
        scores = jnp.where(low, dot(firsts, jnp.concatenate([k, k], axis=1), T_DIMS), 0.0)
        mixed = dot(firsts, jnp.concatenate([state, state], axis=1), T_DIMS) + dot(wide(scores), twice(v))
        mixes.append(mixed.astype(bf16))
        sol_high, sol_low = halves(sol)
        dual_high, dual_low = halves(dual)
        back_high, back_low = halves(back)
        outer = dot(
            jnp.concatenate([dual_high, dual_high, dual_low], axis=0),
            jnp.concatenate([sol_high, sol_low, sol_high], axis=0),
            L_DIMS,
        )
        syms.append(outer + outer.T)
        crosses.append(
            dot(
                jnp.concatenate([back_high, back_high, back_low], axis=0),
                jnp.concatenate([sol_high, sol_low, sol_high], axis=0),
                L_DIMS,
            )
        )
    pack(syms + crosses, send_ref)
    mixes = jnp.concatenate(mixes, axis=1)
    for g in range(w_ref.shape[1] // 256):
        lanes = slice(g * 256, (g + 1) * 256)
        part_ref[:, lanes] = dot(mixes, w_s[:, lanes]).astype(bf16)


def alternate(both):
    r = lax.broadcasted_iota(jnp.int32, (256, 256), 0)
    c = lax.broadcasted_iota(jnp.int32, (256, 256), 1)
    source = (r & 1) * 128 + lax.shift_right_logical(r, 1)
    return dot(jnp.where(c == source, 1.0, 0.0).astype(bf16), both).astype(bf16)


def final_kernel(
    k_ref, v_ref, back_ref, sol_ref, dual_ref, suf_ref, grad_q_ref, grad_k_ref, grad_v_ref
):
    mats = unpack(suf_ref)
    up = causal(128, True)
    grads = []
    for h in range(2):
        lanes = slice(h * 128, (h + 1) * 128)
        k, v, back = k_ref[:, lanes], v_ref[:, lanes], back_ref[:, lanes]
        sol, dual = sol_ref[:, lanes], dual_ref[:, lanes]
        sym, cross = mats[h], mats[2 + h]
        kk = jnp.concatenate([k, k], axis=1)
        vv = jnp.concatenate([v, v], axis=1)
        one = wide(jnp.where(up, dot(kk, wide(sol), T_DIMS), 0.0))
        two = wide(jnp.where(up, dot(kk, wide(dual), T_DIMS), 0.0))
        three = wide(jnp.where(up, dot(vv, wide(back), T_DIMS), 0.0))
        sol_b, dual_b, back_b = sol.astype(bf16), dual.astype(bf16), back.astype(bf16)
        grad_k = dot(three, twice(sol_b)) - dot(one, twice(dual_b)) - dot(two, twice(sol_b))
        grad_k = grad_k + dot(v, cross) - dot(k, sym)
        grad_v = dot(one, twice(back_b)) + dot(k, cross, T_DIMS)
        grads.append(jnp.concatenate([dual_b, grad_k.astype(bf16), grad_v.astype(bf16)], axis=1))
    both = alternate(jnp.concatenate(grads, axis=0))
    grad_q_ref[...] = both[:, :128]
    grad_k_ref[...] = both[:, 128:256]
    grad_v_ref[...] = both[:, 256:]


def call(kernel, outs, n_smem=0, n_in=0, scratch=(), flops=0, bytes_accessed=0, vmem=24, hbm=()):
    specs = [pl.BlockSpec(memory_space=pltpu.SMEM)] * n_smem + [pl.BlockSpec(memory_space=pltpu.VMEM)] * n_in
    for i in hbm:
        specs[i] = pl.BlockSpec(memory_space=pltpu.HBM)
    return pl.pallas_call(
        kernel,
        out_shape=[jax.ShapeDtypeStruct(s, d) for s, d in outs],
        in_specs=specs,
        out_specs=[pl.BlockSpec(memory_space=pltpu.VMEM)] * len(outs),
        scratch_shapes=list(scratch),
        compiler_params=pltpu.CompilerParams(vmem_limit_bytes=vmem * 1024 * 1024),
        cost_estimate=pl.CostEstimate(flops=flops, bytes_accessed=bytes_accessed, transcendentals=0),
    )


def local(queries, keys, values, reg, steps, w_out, d_y):
    size_c, head_count, head_size = queries.shape
    width = head_count * head_size
    spans = lax.axis_size(SEQ)
    packed = (spans * ROWS, head_size)
    tokens = (size_c, width)
    pairs = (size_c * head_count, head_size)
    heads = (size_c, head_count, head_size)

    def exchange(a):
        parts = a.reshape(spans, ROWS // 2, 2, head_size).transpose(0, 2, 1, 3)
        moved = lax.all_to_all(parts.reshape(spans, 2, -1), SEQ, 0, 0)
        parts = moved.reshape(spans, 2, ROWS // 2, head_size).transpose(0, 2, 1, 3)
        return parts.reshape(packed)

    def scan(a, later):
        return call(functools.partial(scan_kernel, later), [(packed, bf16)], 0, 1)(a)[0]

    k_pairs, v_pairs = keys.reshape(pairs), values.reshape(pairs)
    (own,) = call(own_kernel, [(packed, bf16)], 0, 2, vmem=56)(k_pairs, v_pairs)
    dy_rows = lax.all_gather(d_y, ("core", "head"), axis=0, tiled=True)
    q, k, v = (a.reshape(tokens) for a in (queries, keys, values))
    cfg = jnp.concatenate([reg, steps[0].astype(f32)]).reshape(1, -1)
    pre = exchange(scan(exchange(own), False))

    sol, dual, part, send, back = call(
        solve_kernel,
        [(tokens, f32), (tokens, f32), ((size_c, w_out.shape[1]), bf16), (packed, bf16), (tokens, f32)],
        0,
        7,
        [
            pltpu.VMEM((2, 256, 128), f32),
            pltpu.VMEM((2, 256, 128), f32),
            pltpu.VMEM((2, 256, 128), f32),
            pltpu.VMEM((2, 256, 256), bf16),
            pltpu.VMEM((2, 256, 128), bf16),
            pltpu.VMEM((size_c, w_out.shape[1]), bf16),
            pltpu.VMEM(w_out.shape, bf16),
            pltpu.SemaphoreType.DMA((2,)),
        ],
        hbm=(4, 6),
        vmem=53,
        flops=2 * 10**9,
    )(cfg, q, k, v, dy_rows, pre, w_out)
    out = lax.psum_scatter(part, "head", scatter_dimension=0, tiled=True)
    suf = exchange(scan(exchange(send), True))
    grad_q, grad_k, grad_v = call(final_kernel, [(pairs, bf16)] * 3, 0, 6)(
        k, v, back, sol, dual, suf
    )
    return out, grad_q.reshape(heads), grad_k.reshape(heads), grad_v.reshape(heads)


def solution(mesh):
    spans, groups = mesh.devices.shape
    apart = Mesh(mesh.devices.reshape(spans // 2, 2, groups), SEQ + ("head",))
    placed = (
        P(SEQ, "head", None),
        P(SEQ, "head", None),
        P(SEQ, "head", None),
        P("head"),
        P(SEQ, "head"),
        P("head", None),
        P(SEQ + ("head",), None),
    )
    return jax.shard_map(
        local,
        mesh=apart,
        in_specs=placed,
        out_specs=(
            P(SEQ + ("head",), None),
            P(SEQ, "head", None),
            P(SEQ, "head", None),
            P(SEQ, "head", None),
        ),
        check_vma=False,
    )
```
